32 devices in a mesh: dp: 8 (over z, core), fsdp: 4 (over y, x).
Axes of the slice: x: 2, y: 2, z: 4, core: 2. Of those that a mesh axis runs over, the one named last changes fastest.
Arguments:
- tokens: bfloat16 [1024, 3072], P('dp', 'fsdp'), may hold values from -6 to 6
- weight_blocks: bfloat16 [96, 3, 128, 128], P('fsdp'), may hold values from -0.3125 to 0.3125
- pattern: int32 [96, 3], P('fsdp'), may hold values from 0 to 23, as said below
- grad_out: bfloat16 [1024, 12288], P('dp', 'fsdp'), may hold values from -6 to 6
Outputs:
- projected: bfloat16 [1024, 12288], P('dp', 'fsdp')
- grad_tokens: bfloat16 [1024, 3072], P('dp', 'fsdp')
- grad_weight: float32 [96, 3, 16384], P('fsdp', None, 'dp')
The draws below stay inside these ranges and needn't reach their ends.
Inputs may be any that keep to these rules, and one draw needn't show every extreme that they name: `pattern`: each block-column names 3 different block-rows; every block-row is named by exactly 12 block-columns.
All inputs are finite; a program needn't handle non-finite values.
Results may differ from the reference program's by a relative error of at most 0.001.
Values may be sent and summed in bfloat16 or wider, within the bound.
A program may use at most 64 MiB of HBM per device.

```python
import jax
import jax.numpy as jnp
from jax import lax

D = 3072
F = 12288
BLK = 128
K = 3
RB = 24
FB = 96
TOKENS = 1024


def draw_pattern(key, part):
    first_key, second_key = jax.random.split(jax.random.fold_in(key, 7))
    order = jax.random.permutation(first_key, RB)
    offset = jax.random.randint(second_key, (), 0, RB)
    base = (jnp.arange(FB, dtype=jnp.int32) + offset) % RB
    slots = jnp.arange(K, dtype=jnp.int32)
    rows = order[jnp.bitwise_xor(base[:, None], slots[None, :])]
    return rows.astype(jnp.int32)


def level_of(key, dims, cuts, low, largest):
    loudness, own = 1.0, jax.random.fold_in(key, 6)
    for dim, shards_of in cuts:
        draws = jnp.exp(jax.random.uniform(jax.random.fold_in(own, dim), (shards_of,), jnp.float32, low / len(cuts), largest / len(cuts)))
        loudness = loudness * jnp.repeat(draws, dims[dim] // shards_of).reshape([-1 if axis == dim else 1 for axis in range(len(dims))])
    return loudness


def gaussian(own_key, shape, width, most, shards=(), kind=jnp.bfloat16):
    entries = jax.random.normal(own_key, shape, jnp.float32) * width
    if len(shards) > 0:
        entries = level_of(own_key, shape, shards, -0.22, 0.18) * entries
    return jnp.clip(entries, min=-most, max=most).astype(kind)


def setup_inputs(seed: int = 0) -> dict:
    key_of = jax.random.split(jax.random.key(seed), 5)
    return {
        "tokens": gaussian(key_of[0], (TOKENS, D), 1.0, 6.0, ((0, 8), (1, 4))),
        "weight_blocks": gaussian(key_of[1], (FB, K, BLK, BLK), (K * BLK) ** -0.5, 0.3125, ((0, 4),)),
        "pattern": draw_pattern(jax.random.fold_in(key_of[4], 71), 0),
        "grad_out": gaussian(key_of[3], (TOKENS, F), 1.0, 6.0, ((0, 8), (1, 4))),
    }


def reference(tokens, weight_blocks, pattern, grad_out):
    count_rows = tokens.shape[0]
    token_rows = tokens.reshape(count_rows, RB, BLK)
    grad_cols = jnp.transpose(grad_out.reshape(count_rows, FB, BLK), (1, 0, 2))

    def column_step(carry, inputs):
        rows, weights, grad_block = inputs
        picked = jnp.take(token_rows, rows, axis=1).astype(jnp.float32)
        weights_wide = weights.astype(jnp.float32)
        grad_wide = grad_block.astype(jnp.float32)
        output_block = jnp.einsum('tkb,kbo->to', picked, weights_wide).astype(jnp.bfloat16)
        backward = jnp.einsum('to,kbo->tkb', grad_wide, weights_wide)
        carry = carry.at[:, rows].add(backward)
        weight_grad = jnp.einsum('tkb,to->kbo', picked, grad_wide)
        return (carry, (output_block, weight_grad))
    start = jnp.zeros((count_rows, RB, BLK), jnp.float32)
    summed, (outputs, weight_grads) = lax.scan(column_step, start, (pattern, weight_blocks, grad_cols))
    projected = jnp.transpose(outputs, (1, 0, 2)).reshape(count_rows, FB * BLK)
    grad_tokens = summed.reshape(count_rows, D).astype(jnp.bfloat16)
    grad_weight = (weight_grads / jnp.sqrt(jnp.float32(TOKENS))).reshape(FB, K, BLK * BLK)
    return (projected, grad_tokens, grad_weight)
```

```python
import functools

import jax
import jax.numpy as jnp
from jax import lax
from jax.experimental import pallas as pl
from jax.experimental.pallas import tpu as pltpu
from jax.sharding import PartitionSpec as P

MESH = pl.DeviceIdType.MESH
LEVELS = 32766.0


def plain(tokens, weight_blocks, pattern, grad_out):
    count_rows = tokens.shape[0]
    columns, slots, block_size = (
        weight_blocks.shape[0],
        weight_blocks.shape[1],
        weight_blocks.shape[3],
    )
    whole = lax.all_gather(tokens, "fsdp", axis=1, tiled=True)
    width = whole.shape[1]
    row_blocks = width // block_size
    whole_rows = whole.reshape(count_rows, row_blocks, block_size)
    grad_cols = grad_out.reshape(count_rows, columns, block_size)
    row_ids = jnp.arange(row_blocks, dtype=jnp.int32)
    projected_sum = jnp.zeros((count_rows, columns, block_size), jnp.float32)
    partial_grads = jnp.zeros((count_rows, row_blocks, block_size), jnp.float32)
    slot_terms = []
    for slot in range(slots):
        selector = row_ids[:, None] == pattern[:, slot][None, :]
        picked_slot = jnp.einsum(
            "trb,rc->tcb",
            whole_rows,
            selector.astype(jnp.bfloat16),
            preferred_element_type=jnp.float32,
        ).astype(jnp.bfloat16)
        weight_slot = weight_blocks[:, slot]
        projected_sum = projected_sum + jnp.einsum(
            "tcb,cbo->tco", picked_slot, weight_slot, preferred_element_type=jnp.float32
        )
        backward_slot = jnp.einsum(
            "tco,cbo->tcb", grad_cols, weight_slot, preferred_element_type=jnp.float32
        )
        partial_grads = partial_grads + jnp.einsum(
            "tcb,rc->trb",
            backward_slot,
            selector.astype(jnp.float32),
            precision=lax.Precision.HIGHEST,
        )
        slot_terms.append(
            jnp.einsum(
                "tcb,tco->cbo", picked_slot, grad_cols, preferred_element_type=jnp.float32
            ).reshape(columns, block_size * block_size)
        )
    projected = projected_sum.astype(jnp.bfloat16).reshape(count_rows, columns * block_size)
    partial_grads = partial_grads.reshape(count_rows, width)
    grad_tokens = lax.psum_scatter(partial_grads, "fsdp", scatter_dimension=1, tiled=True).astype(
        jnp.bfloat16
    )
    scale_factor = 1.0 / jnp.sqrt(jnp.float32(count_rows * lax.axis_size("dp")))
    weight_terms = jnp.stack(slot_terms, axis=1)
    grad_weight = (
        lax.psum_scatter(weight_terms, "dp", scatter_dimension=2, tiled=True) * scale_factor
    )
    return (projected, grad_tokens, grad_weight)


def kernel(
    nf, nz, group, factor,
    pat, prev, tok, w_hbm, g_hbm,
    out_p, out_t, out_w,
    x_all, xb, xt, xt_sib, g_own, g_sib, w, acc, part, part_in, terms, q_out, q_in, s_out, s_in,
    local_sem, ag_send, ag_recv, sib_send, sib_recv, rs_send, rs_recv, z_send, z_recv, s_send, s_recv,
):
    d = lax.axis_index("dp")
    f = lax.axis_index("fsdp")
    z = d // 2
    core = lax.rem(d, 2)
    sib = (z * 2 + 1 - core, f)
    columns, slots, blk, _ = w.shape
    entries = columns * slots
    row_blocks = xb.shape[0]
    per = row_blocks // nf
    chunks = columns // group

    def peer_f(j):
        return lax.rem(f + j, nf)

    def peer_z(j):
        return lax.rem(z + j, nz)

    local = [
        pltpu.make_async_copy(g_hbm, g_own, local_sem.at[0]),
        pltpu.make_async_copy(w_hbm, w, local_sem.at[1]),
        pltpu.make_async_copy(tok, x_all.at[f], local_sem.at[2]),
    ]
    for copy in local:
        copy.start()

    barrier = pltpu.get_barrier_semaphore()
    for j in range(1, nf):
        pl.semaphore_signal(barrier, inc=1, device_id=(d, peer_f(j)), device_id_type=MESH)
    for j in range(1, nz):
        pl.semaphore_signal(
            barrier, inc=1, device_id=(peer_z(j) * 2 + core, f), device_id_type=MESH
        )
    pl.semaphore_signal(barrier, inc=1, device_id=sib, device_id_type=MESH)
    pl.semaphore_wait(barrier, nf + nz - 1)

    gather = [
        pltpu.make_async_remote_copy(
            tok, x_all.at[f], ag_send.at[j - 1], ag_recv.at[j - 1],
            device_id=(d, peer_f(j)), device_id_type=MESH,
        )
        for j in range(1, nf)
    ]
    for copy in gather:
        copy.start()
    g_swap = pltpu.make_async_remote_copy(
        g_hbm, g_sib, sib_send.at[0], sib_recv.at[0], device_id=sib, device_id_type=MESH
    )
    g_swap.start()

    acc[entries] = jnp.zeros((blk, blk), jnp.float32)
    local[0].wait()
    local[1].wait()

    def lanes(c):
        return pl.ds(pl.multiple_of(c * blk, blk), blk)

    def backward(c):
        terms_c = lax.dot_general(
            g_own[:, lanes(c)], w[c].reshape(slots * blk, blk),
            (((1,), (1,)), ((), ())), preferred_element_type=jnp.float32,
        )
        for k in range(slots):
            e = c * slots + k
            acc[e] = terms_c[:, k * blk:(k + 1) * blk] + acc[prev[e]]

    @pl.loop(0, columns // 2)
    def _(i):
        backward(i * 2)
        backward(i * 2 + 1)

    for j in range(nf):
        to = peer_f(j)
        for i in range(per):
            part[j, :, i * blk:(i + 1) * blk] = acc[prev[entries + to * per + i]]

    local[2].wait()
    for copy in gather:
        copy.wait_recv()

    scatter = [
        pltpu.make_async_remote_copy(
            part.at[j], part_in.at[j - 1], rs_send.at[j - 1], rs_recv.at[j - 1],
            device_id=(d, peer_f(j)), device_id_type=MESH,
        )
        for j in range(1, nf)
    ]
    rows = xt.shape[3]
    for r in range(row_blocks):
        block = x_all[r // per, :, (r % per) * blk:(r % per + 1) * blk]
        xb[r] = block
        xt[r] = block.T.reshape(nz, 2, rows, blk)
    x_swap = pltpu.make_async_remote_copy(
        xt.at[:, :, 1 - core], xt_sib, sib_send.at[1], sib_recv.at[1],
        device_id=sib, device_id_type=MESH,
    )
    x_swap.start()
    for copy in scatter:
        copy.start()
    g_swap.wait_recv()
    x_swap.wait_recv()

    def z_copies(n, j):
        where = (peer_z(j) * 2 + core, f)
        return (
            pltpu.make_async_remote_copy(
                q_out.at[peer_z(j), n], q_in.at[j - 1, n],
                z_send.at[j - 1, n], z_recv.at[j - 1, n],
                device_id=where, device_id_type=MESH,
            ),
            pltpu.make_async_remote_copy(
                s_out.at[peer_z(j), n], s_in.at[j - 1, n],
                s_send.at[j - 1, n], s_recv.at[j - 1, n],
                device_id=where, device_id_type=MESH,
            ),
        )

    @pl.loop(0, chunks)
    def _(n):
        for i in range(group):
            c = n * group + i
            lhs = jnp.concatenate(
                [
                    jnp.concatenate(
                        [
                            xt[pat[c, k], :, core].reshape(nz * rows, blk),
                            xt_sib[pat[c, k]].reshape(nz * rows, blk),
                        ],
                        axis=1,
                    )
                    for k in range(slots)
                ],
                axis=0,
            )
            rhs = jnp.concatenate([g_own[:, lanes(c)], g_sib[:, lanes(c)]], axis=0)
            sums = jnp.dot(lhs, rhs, preferred_element_type=jnp.float32)
            sums = sums.reshape(slots, nz, rows, blk)
            for v in range(nz):
                mine = sums[:, v]
                terms[c, v] = mine
                top = jnp.max(jnp.max(jnp.abs(mine), axis=0), axis=0, keepdims=True)
                top = jnp.maximum(top, 1e-30)
                s_out[v, n, i:i + 1] = top * (1.0 / LEVELS)
                coded = jnp.round(mine * (LEVELS / top))
                q_out[v, n, i] = coded.astype(jnp.int32).astype(jnp.int16)
        for j in range(1, nz):
            for copy in z_copies(n, j):
                copy.start()

    def forward(c):
        lhs = jnp.concatenate([xb[pat[c, k]] for k in range(slots)], axis=1)
        total = jnp.dot(
            lhs, w[c].reshape(slots * blk, blk), preferred_element_type=jnp.float32
        )
        out_p[:, lanes(c)] = total.astype(out_p.dtype)

    @pl.loop(0, columns // 2)
    def _(i):
        forward(i * 2)
        forward(i * 2 + 1)

    for copy in scatter:
        copy.wait_recv()
    total = part[0]
    for j in range(nf - 1):
        total = total + part_in[j]
    out_t[...] = total.astype(out_t.dtype)

    @pl.loop(0, chunks)
    def _(n):
        for j in range(1, nz):
            for copy in z_copies(n, j):
                copy.wait_recv()
        for i in range(group):
            c = n * group + i
            total = terms[c, z]
            for j in range(nz - 1):
                coded = q_in[j, n, i].astype(jnp.int32).astype(jnp.float32)
                total = total + coded * s_in[j, n, i:i + 1].reshape(1, 1, blk)
            out_w[c] = total * factor

    for copy in gather + scatter + [g_swap, x_swap]:
        copy.wait_send()

    @pl.loop(0, chunks)
    def _(n):
        for j in range(1, nz):
            for copy in z_copies(n, j):
                copy.wait_send()


def fused(nd, nf, tokens, weight_blocks, pattern, grad_out):
    count, width = tokens.shape
    columns, slots, blk, _ = weight_blocks.shape
    row_blocks = width * nf // blk
    entries = columns * slots
    nz = nd // 2
    rows = blk // nd
    group = 4
    chunks = columns // group
    flat = pattern.reshape(entries)
    ids = jnp.arange(entries, dtype=jnp.int32)
    keys = jnp.concatenate([flat, jnp.arange(row_blocks, dtype=jnp.int32)])
    limit = jnp.concatenate([ids, jnp.full((row_blocks,), entries, jnp.int32)])
    found = (flat[None, :] == keys[:, None]) & (ids[None, :] < limit[:, None])
    last = jnp.max(jnp.where(found, ids[None, :], -1), axis=1)
    prev = jnp.where(last < 0, entries, last)
    vmem = pl.BlockSpec(memory_space=pltpu.VMEM)
    smem = pl.BlockSpec(memory_space=pltpu.SMEM)
    hbm = pl.BlockSpec(memory_space=pl.ANY)
    dma = pltpu.SemaphoreType.DMA
    bf, f32 = jnp.bfloat16, jnp.float32
    projected, grad_tokens, grad_weight = pl.pallas_call(
        functools.partial(kernel, nf, nz, group, float((count * nd) ** -0.5)),
        out_shape=(
            jax.ShapeDtypeStruct((count, columns * blk), bf),
            jax.ShapeDtypeStruct((count, width), bf),
            jax.ShapeDtypeStruct((columns, slots, rows, blk), f32),
        ),
        in_specs=[smem, smem, hbm, hbm, hbm],
        out_specs=(vmem, vmem, vmem),
        scratch_shapes=[
            pltpu.VMEM((nf, count, width), bf),
            pltpu.VMEM((row_blocks, count, blk), bf),
            pltpu.VMEM((row_blocks, nz, 2, rows, count), bf),
            pltpu.VMEM((row_blocks, nz, rows, count), bf),
            pltpu.VMEM((count, columns * blk), bf),
            pltpu.VMEM((count, columns * blk), bf),
            pltpu.VMEM((columns, slots, blk, blk), bf),
            pltpu.VMEM((entries + 1, count, blk), f32),
            pltpu.VMEM((nf, count, width), f32),
            pltpu.VMEM((nf - 1, count, width), f32),
            pltpu.VMEM((columns, nz, slots, rows, blk), f32),
            pltpu.VMEM((nz, chunks, group, slots, rows, blk), jnp.int16),
            pltpu.VMEM((nz - 1, chunks, group, slots, rows, blk), jnp.int16),
            pltpu.VMEM((nz, chunks, 8, blk), f32),
            pltpu.VMEM((nz - 1, chunks, 8, blk), f32),
            dma((3,)),
            dma((nf - 1,)), dma((nf - 1,)),
            dma((2,)), dma((2,)),
            dma((nf - 1,)), dma((nf - 1,)),
            dma((nz - 1, chunks)), dma((nz - 1, chunks)),
            dma((nz - 1, chunks)), dma((nz - 1, chunks)),
        ],
        compiler_params=pltpu.CompilerParams(
            collective_id=0, has_side_effects=True, vmem_limit_bytes=40 * 1024 * 1024
        ),
    )(pattern, prev, tokens, weight_blocks, grad_out)
    return projected, grad_tokens, grad_weight.reshape(columns, slots, rows * blk)


def solution(mesh):
    nd, nf = mesh.shape["dp"], mesh.shape["fsdp"]
    placed = (P("dp", "fsdp"), P("fsdp", None, None, None), P("fsdp", None), P("dp", "fsdp"))

    def on_device(tokens, weight_blocks, pattern, grad_out):
        columns, slots, blk, _ = weight_blocks.shape
        fits = (
            nd % 2 == 0 and 4 <= nd and blk % (16 * nd) == 0 and blk == 128
            and tokens.shape[0] == blk and columns % 4 == 0 and nf > 1
        )
        if fits:
            return fused(nd, nf, tokens, weight_blocks, pattern, grad_out)
        return plain(tokens, weight_blocks, pattern, grad_out)

    return jax.shard_map(
        on_device,
        mesh=mesh,
        in_specs=placed,
        out_specs=(P("dp", "fsdp"), P("dp", "fsdp"), P("fsdp", None, "dp")),
        check_vma=False,
    )
```

```python
import functools

import jax
import jax.numpy as jnp
from jax import lax
from jax.experimental import pallas as pl
from jax.experimental.pallas import tpu as pltpu
from jax.sharding import PartitionSpec as P

MESH = pl.DeviceIdType.MESH
LEVELS = 32766.0


def plain(tokens, weight_blocks, pattern, grad_out):
    count_rows = tokens.shape[0]
    columns, slots, block_size = (
        weight_blocks.shape[0],
        weight_blocks.shape[1],
        weight_blocks.shape[3],
    )
    whole = lax.all_gather(tokens, "fsdp", axis=1, tiled=True)
    width = whole.shape[1]
    row_blocks = width // block_size
    whole_rows = whole.reshape(count_rows, row_blocks, block_size)
    grad_cols = grad_out.reshape(count_rows, columns, block_size)
    row_ids = jnp.arange(row_blocks, dtype=jnp.int32)
    projected_sum = jnp.zeros((count_rows, columns, block_size), jnp.float32)
    partial_grads = jnp.zeros((count_rows, row_blocks, block_size), jnp.float32)
    slot_terms = []
    for slot in range(slots):
        selector = row_ids[:, None] == pattern[:, slot][None, :]
        picked_slot = jnp.einsum(
            "trb,rc->tcb",
            whole_rows,
            selector.astype(jnp.bfloat16),
            preferred_element_type=jnp.float32,
        ).astype(jnp.bfloat16)
        weight_slot = weight_blocks[:, slot]
        projected_sum = projected_sum + jnp.einsum(
            "tcb,cbo->tco", picked_slot, weight_slot, preferred_element_type=jnp.float32
        )
        backward_slot = jnp.einsum(
            "tco,cbo->tcb", grad_cols, weight_slot, preferred_element_type=jnp.float32
        )
        partial_grads = partial_grads + jnp.einsum(
            "tcb,rc->trb",
            backward_slot,
            selector.astype(jnp.float32),
            precision=lax.Precision.HIGHEST,
        )
        slot_terms.append(
            jnp.einsum(
                "tcb,tco->cbo", picked_slot, grad_cols, preferred_element_type=jnp.float32
            ).reshape(columns, block_size * block_size)
        )
    projected = projected_sum.astype(jnp.bfloat16).reshape(count_rows, columns * block_size)
    partial_grads = partial_grads.reshape(count_rows, width)
    grad_tokens = lax.psum_scatter(partial_grads, "fsdp", scatter_dimension=1, tiled=True).astype(
        jnp.bfloat16
    )
    scale_factor = 1.0 / jnp.sqrt(jnp.float32(count_rows * lax.axis_size("dp")))
    weight_terms = jnp.stack(slot_terms, axis=1)
    grad_weight = (
        lax.psum_scatter(weight_terms, "dp", scatter_dimension=2, tiled=True) * scale_factor
    )
    return (projected, grad_tokens, grad_weight)


def kernel(
    nf, nz, group, factor,
    pat, prev, tok, w_hbm, g_hbm,
    out_p, out_t, out_w,
    x_all, xb, xt, xt_sib, g_own, g_sib, w, acc, part, part_in, terms, q_out, q_in, s_out, s_in,
    local_sem, ag_send, ag_recv, sib_send, sib_recv, rs_send, rs_recv, z_send, z_recv, s_send, s_recv,
):
    d = lax.axis_index("dp")
    f = lax.axis_index("fsdp")
    z = d // 2
    core = lax.rem(d, 2)
    sib = (z * 2 + 1 - core, f)
    columns, slots, blk, _ = w.shape
    entries = columns * slots
    row_blocks = xb.shape[0]
    per = row_blocks // nf
    chunks = columns // group

    def peer_f(j):
        return lax.rem(f + j, nf)

    def peer_z(j):
        return lax.rem(z + j, nz)

    local = [
        pltpu.make_async_copy(g_hbm, g_own, local_sem.at[0]),
        pltpu.make_async_copy(w_hbm, w, local_sem.at[1]),
        pltpu.make_async_copy(tok, x_all.at[f], local_sem.at[2]),
    ]
    for copy in local:
        copy.start()

    barrier = pltpu.get_barrier_semaphore()
    for j in range(1, nf):
        pl.semaphore_signal(barrier, inc=1, device_id=(d, peer_f(j)), device_id_type=MESH)
    for j in range(1, nz):
        pl.semaphore_signal(
            barrier, inc=1, device_id=(peer_z(j) * 2 + core, f), device_id_type=MESH
        )
    pl.semaphore_signal(barrier, inc=1, device_id=sib, device_id_type=MESH)
    pl.semaphore_wait(barrier, nf + nz - 1)

    gather = [
        pltpu.make_async_remote_copy(
            tok, x_all.at[f], ag_send.at[j - 1], ag_recv.at[j - 1],
            device_id=(d, peer_f(j)), device_id_type=MESH,
        )
        for j in range(1, nf)
    ]
    for copy in gather:
        copy.start()
    g_swap = pltpu.make_async_remote_copy(
        g_hbm, g_sib, sib_send.at[0], sib_recv.at[0], device_id=sib, device_id_type=MESH
    )
    g_swap.start()

    acc[entries] = jnp.zeros((blk, blk), jnp.float32)
    local[0].wait()
    local[1].wait()

    def lanes(c):
        return pl.ds(pl.multiple_of(c * blk, blk), blk)

    def backward(c):
        terms_c = lax.dot_general(
            g_own[:, lanes(c)], w[c].reshape(slots * blk, blk),
            (((1,), (1,)), ((), ())), preferred_element_type=jnp.float32,
        )
        for k in range(slots):
            e = c * slots + k
            acc[e] = terms_c[:, k * blk:(k + 1) * blk] + acc[prev[e]]

    @pl.loop(0, columns // 2)
    def _(i):
        backward(i * 2)
        backward(i * 2 + 1)

    for j in range(nf):
        to = peer_f(j)
        for i in range(per):
            part[j, :, i * blk:(i + 1) * blk] = acc[prev[entries + to * per + i]]

    local[2].wait()
    for copy in gather:
        copy.wait_recv()

    scatter = [
        pltpu.make_async_remote_copy(
            part.at[j], part_in.at[j - 1], rs_send.at[j - 1], rs_recv.at[j - 1],
            device_id=(d, peer_f(j)), device_id_type=MESH,
        )
        for j in range(1, nf)
    ]
    rows = xt.shape[3]
    for r in range(row_blocks):
        block = x_all[r // per, :, (r % per) * blk:(r % per + 1) * blk]
        xb[r] = block
        xt[r] = block.T.reshape(nz, 2, rows, blk)
    x_swap = pltpu.make_async_remote_copy(
        xt.at[:, :, 1 - core], xt_sib, sib_send.at[1], sib_recv.at[1],
        device_id=sib, device_id_type=MESH,
    )
    x_swap.start()
    for copy in scatter:
        copy.start()
    g_swap.wait_recv()
    x_swap.wait_recv()

    def z_copies(n, j):
        where = (peer_z(j) * 2 + core, f)
        return (
            pltpu.make_async_remote_copy(
                q_out.at[peer_z(j), n], q_in.at[j - 1, n],
                z_send.at[j - 1, n], z_recv.at[j - 1, n],
                device_id=where, device_id_type=MESH,
            ),
            pltpu.make_async_remote_copy(
                s_out.at[peer_z(j), n], s_in.at[j - 1, n],
                s_send.at[j - 1, n], s_recv.at[j - 1, n],
                device_id=where, device_id_type=MESH,
            ),
        )

    @pl.loop(0, chunks)
    def _(n):
        for i in range(group):
            c = n * group + i
            lhs = jnp.concatenate(
                [
                    jnp.concatenate(
                        [
                            xt[pat[c, k], :, core].reshape(nz * rows, blk),
                            xt_sib[pat[c, k]].reshape(nz * rows, blk),
                        ],
                        axis=1,
                    )
                    for k in range(slots)
                ],
                axis=0,
            )
            rhs = jnp.concatenate([g_own[:, lanes(c)], g_sib[:, lanes(c)]], axis=0)
            sums = jnp.dot(lhs, rhs, preferred_element_type=jnp.float32)
            sums = sums.reshape(slots, nz, rows, blk)
            for v in range(nz):
                mine = sums[:, v]
                terms[c, v] = mine
                top = jnp.max(jnp.max(jnp.abs(mine), axis=0), axis=0, keepdims=True)
                top = jnp.maximum(top, 1e-30)
                s_out[v, n, i:i + 1] = top * (1.0 / LEVELS)
                coded = jnp.round(mine * (LEVELS / top))
                q_out[v, n, i] = coded.astype(jnp.int32).astype(jnp.int16)
        for j in sorted(range(1, nz), key=lambda j: abs(2 * j - nz)):
            for copy in z_copies(n, j):
                copy.start()

    def forward(c):
        lhs = jnp.concatenate([xb[pat[c, k]] for k in range(slots)], axis=1)
        total = jnp.dot(
            lhs, w[c].reshape(slots * blk, blk), preferred_element_type=jnp.float32
        )
        out_p[:, lanes(c)] = total.astype(out_p.dtype)

    @pl.loop(0, columns // 2)
    def _(i):
        forward(i * 2)
        forward(i * 2 + 1)

    for copy in scatter:
        copy.wait_recv()
    total = part[0]
    for j in range(nf - 1):
        total = total + part_in[j]
    out_t[...] = total.astype(out_t.dtype)

    @pl.loop(0, chunks)
    def _(n):
        for j in range(1, nz):
            for copy in z_copies(n, j):
                copy.wait_recv()
        for i in range(group):
            c = n * group + i
            total = terms[c, z]
            for j in range(nz - 1):
                coded = q_in[j, n, i].astype(jnp.int32).astype(jnp.float32)
                total = total + coded * s_in[j, n, i:i + 1].reshape(1, 1, blk)
            out_w[c] = total * factor

    for copy in gather + scatter + [g_swap, x_swap]:
        copy.wait_send()

    @pl.loop(0, chunks)
    def _(n):
        for j in range(1, nz):
            for copy in z_copies(n, j):
                copy.wait_send()


def fused(nd, nf, tokens, weight_blocks, pattern, grad_out):
    count, width = tokens.shape
    columns, slots, blk, _ = weight_blocks.shape
    row_blocks = width * nf // blk
    entries = columns * slots
    nz = nd // 2
    rows = blk // nd
    group = 4
    chunks = columns // group
    flat = pattern.reshape(entries)
    ids = jnp.arange(entries, dtype=jnp.int32)
    keys = jnp.concatenate([flat, jnp.arange(row_blocks, dtype=jnp.int32)])
    limit = jnp.concatenate([ids, jnp.full((row_blocks,), entries, jnp.int32)])
    found = (flat[None, :] == keys[:, None]) & (ids[None, :] < limit[:, None])
    last = jnp.max(jnp.where(found, ids[None, :], -1), axis=1)
    prev = jnp.where(last < 0, entries, last)
    vmem = pl.BlockSpec(memory_space=pltpu.VMEM)
    smem = pl.BlockSpec(memory_space=pltpu.SMEM)
    hbm = pl.BlockSpec(memory_space=pl.ANY)
    dma = pltpu.SemaphoreType.DMA
    bf, f32 = jnp.bfloat16, jnp.float32
    projected, grad_tokens, grad_weight = pl.pallas_call(
        functools.partial(kernel, nf, nz, group, float((count * nd) ** -0.5)),
        out_shape=(
            jax.ShapeDtypeStruct((count, columns * blk), bf),
            jax.ShapeDtypeStruct((count, width), bf),
            jax.ShapeDtypeStruct((columns, slots, rows, blk), f32),
        ),
        in_specs=[smem, smem, hbm, hbm, hbm],
        out_specs=(vmem, vmem, vmem),
        scratch_shapes=[
            pltpu.VMEM((nf, count, width), bf),
            pltpu.VMEM((row_blocks, count, blk), bf),
            pltpu.VMEM((row_blocks, nz, 2, rows, count), bf),
            pltpu.VMEM((row_blocks, nz, rows, count), bf),
            pltpu.VMEM((count, columns * blk), bf),
            pltpu.VMEM((count, columns * blk), bf),
            pltpu.VMEM((columns, slots, blk, blk), bf),
            pltpu.VMEM((entries + 1, count, blk), f32),
            pltpu.VMEM((nf, count, width), f32),
            pltpu.VMEM((nf - 1, count, width), f32),
            pltpu.VMEM((columns, nz, slots, rows, blk), f32),
            pltpu.VMEM((nz, chunks, group, slots, rows, blk), jnp.int16),
            pltpu.VMEM((nz - 1, chunks, group, slots, rows, blk), jnp.int16),
            pltpu.VMEM((nz, chunks, 8, blk), f32),
            pltpu.VMEM((nz - 1, chunks, 8, blk), f32),
            dma((3,)),
            dma((nf - 1,)), dma((nf - 1,)),
            dma((2,)), dma((2,)),
            dma((nf - 1,)), dma((nf - 1,)),
            dma((nz - 1, chunks)), dma((nz - 1, chunks)),
            dma((nz - 1, chunks)), dma((nz - 1, chunks)),
        ],
        compiler_params=pltpu.CompilerParams(
            collective_id=0, has_side_effects=True, vmem_limit_bytes=60 * 1024 * 1024
        ),
    )(pattern, prev, tokens, weight_blocks, grad_out)
    return projected, grad_tokens, grad_weight.reshape(columns, slots, rows * blk)


def solution(mesh):
    nd, nf = mesh.shape["dp"], mesh.shape["fsdp"]
    placed = (P("dp", "fsdp"), P("fsdp", None, None, None), P("fsdp", None), P("dp", "fsdp"))

    def on_device(tokens, weight_blocks, pattern, grad_out):
        columns, slots, blk, _ = weight_blocks.shape
        fits = (
            nd % 2 == 0 and 4 <= nd and blk % (16 * nd) == 0 and blk == 128
            and tokens.shape[0] == blk and columns % 4 == 0 and nf > 1
        )
        if fits:
            return fused(nd, nf, tokens, weight_blocks, pattern, grad_out)
        return plain(tokens, weight_blocks, pattern, grad_out)

    return jax.shard_map(
        on_device,
        mesh=mesh,
        in_specs=placed,
        out_specs=(P("dp", "fsdp"), P("dp", "fsdp"), P("fsdp", None, "dp")),
        check_vma=False,
    )
```

```python
import functools

import jax
import jax.numpy as jnp
from jax import lax
from jax.experimental import pallas as pl
from jax.experimental.pallas import tpu as pltpu
from jax.sharding import PartitionSpec as P

MESH = pl.DeviceIdType.MESH
LEVELS = 32766.0


def plain(tokens, weight_blocks, pattern, grad_out):
    count_rows = tokens.shape[0]
    columns, slots, block_size = (
        weight_blocks.shape[0],
        weight_blocks.shape[1],
        weight_blocks.shape[3],
    )
    whole = lax.all_gather(tokens, "fsdp", axis=1, tiled=True)
    width = whole.shape[1]
    row_blocks = width // block_size
    whole_rows = whole.reshape(count_rows, row_blocks, block_size)
    grad_cols = grad_out.reshape(count_rows, columns, block_size)
    row_ids = jnp.arange(row_blocks, dtype=jnp.int32)
    projected_sum = jnp.zeros((count_rows, columns, block_size), jnp.float32)
    partial_grads = jnp.zeros((count_rows, row_blocks, block_size), jnp.float32)
    slot_terms = []
    for slot in range(slots):
        selector = row_ids[:, None] == pattern[:, slot][None, :]
        picked_slot = jnp.einsum(
            "trb,rc->tcb",
            whole_rows,
            selector.astype(jnp.bfloat16),
            preferred_element_type=jnp.float32,
        ).astype(jnp.bfloat16)
        weight_slot = weight_blocks[:, slot]
        projected_sum = projected_sum + jnp.einsum(
            "tcb,cbo->tco", picked_slot, weight_slot, preferred_element_type=jnp.float32
        )
        backward_slot = jnp.einsum(
            "tco,cbo->tcb", grad_cols, weight_slot, preferred_element_type=jnp.float32
        )
        partial_grads = partial_grads + jnp.einsum(
            "tcb,rc->trb",
            backward_slot,
            selector.astype(jnp.float32),
            precision=lax.Precision.HIGHEST,
        )
        slot_terms.append(
            jnp.einsum(
                "tcb,tco->cbo", picked_slot, grad_cols, preferred_element_type=jnp.float32
            ).reshape(columns, block_size * block_size)
        )
    projected = projected_sum.astype(jnp.bfloat16).reshape(count_rows, columns * block_size)
    partial_grads = partial_grads.reshape(count_rows, width)
    grad_tokens = lax.psum_scatter(partial_grads, "fsdp", scatter_dimension=1, tiled=True).astype(
        jnp.bfloat16
    )
    scale_factor = 1.0 / jnp.sqrt(jnp.float32(count_rows * lax.axis_size("dp")))
    weight_terms = jnp.stack(slot_terms, axis=1)
    grad_weight = (
        lax.psum_scatter(weight_terms, "dp", scatter_dimension=2, tiled=True) * scale_factor
    )
    return (projected, grad_tokens, grad_weight)


def kernel(
    nf, nz, group, factor,
    pat, prev, tok, w_hbm, g_hbm,
    out_p, out_t, out_w,
    x_all, xb, xt, xt_sib, g_own, g_sib, w, acc, part, part_in, terms, q_out, q_in, s_out, s_in, q_mid, s_mid,
    local_sem, ag_send, ag_recv, sib_send, sib_recv, rs_send, rs_recv, z_send, z_recv, s_send, s_recv,
    m_send, m_recv,
):
    d = lax.axis_index("dp")
    f = lax.axis_index("fsdp")
    z = d // 2
    core = lax.rem(d, 2)
    sib = (z * 2 + 1 - core, f)
    columns, slots, blk, _ = w.shape
    entries = columns * slots
    row_blocks = xb.shape[0]
    per = row_blocks // nf
    chunks = columns // group

    def peer_f(j):
        return lax.rem(f + j, nf)

    def peer_z(j):
        return lax.rem(z + j, nz)

    local = [
        pltpu.make_async_copy(g_hbm, g_own, local_sem.at[0]),
        pltpu.make_async_copy(w_hbm, w, local_sem.at[1]),
        pltpu.make_async_copy(tok, x_all.at[f], local_sem.at[2]),
    ]
    for copy in local:
        copy.start()

    barrier = pltpu.get_barrier_semaphore()
    for j in range(1, nf):
        pl.semaphore_signal(barrier, inc=1, device_id=(d, peer_f(j)), device_id_type=MESH)
    for j in range(1, nz):
        pl.semaphore_signal(
            barrier, inc=1, device_id=(peer_z(j) * 2 + core, f), device_id_type=MESH
        )
    pl.semaphore_signal(barrier, inc=1, device_id=sib, device_id_type=MESH)
    pl.semaphore_wait(barrier, nf + nz - 1)

    gather = [
        pltpu.make_async_remote_copy(
            tok, x_all.at[f], ag_send.at[j - 1], ag_recv.at[j - 1],
            device_id=(d, peer_f(j)), device_id_type=MESH,
        )
        for j in range(1, nf)
    ]
    for copy in gather:
        copy.start()
    g_swap = pltpu.make_async_remote_copy(
        g_hbm, g_sib, sib_send.at[0], sib_recv.at[0], device_id=sib, device_id_type=MESH
    )
    g_swap.start()

    acc[entries] = jnp.zeros((blk, blk), jnp.float32)
    local[0].wait()
    local[1].wait()

    def lanes(c):
        return pl.ds(pl.multiple_of(c * blk, blk), blk)

    def backward(c):
        terms_c = lax.dot_general(
            g_own[:, lanes(c)], w[c].reshape(slots * blk, blk),
            (((1,), (1,)), ((), ())), preferred_element_type=jnp.float32,
        )
        for k in range(slots):
            e = c * slots + k
            acc[e] = terms_c[:, k * blk:(k + 1) * blk] + acc[prev[e]]

    @pl.loop(0, columns // 2)
    def _(i):
        backward(i * 2)
        backward(i * 2 + 1)

    for j in range(nf):
        to = peer_f(j)
        for i in range(per):
            part[j, :, i * blk:(i + 1) * blk] = acc[prev[entries + to * per + i]]

    local[2].wait()
    for copy in gather:
        copy.wait_recv()

    scatter = [
        pltpu.make_async_remote_copy(
            part.at[j], part_in.at[j - 1], rs_send.at[j - 1], rs_recv.at[j - 1],
            device_id=(d, peer_f(j)), device_id_type=MESH,
        )
        for j in range(1, nf)
    ]
    rows = xt.shape[3]
    for r in range(row_blocks):
        block = x_all[r // per, :, (r % per) * blk:(r % per + 1) * blk]
        xb[r] = block
        xt[r] = block.T.reshape(nz, 2, rows, blk)
    x_swap = pltpu.make_async_remote_copy(
        xt.at[:, :, 1 - core], xt_sib, sib_send.at[1], sib_recv.at[1],
        device_id=sib, device_id_type=MESH,
    )
    x_swap.start()
    for copy in scatter:
        copy.start()
    g_swap.wait_recv()
    x_swap.wait_recv()

    def z_copies(n, j):
        where = (peer_z(j) * 2 + core, f)
        return (
            pltpu.make_async_remote_copy(
                q_out.at[peer_z(j), n], q_in.at[j - 1, n],
                z_send.at[j - 1, n], z_recv.at[j - 1, n],
                device_id=where, device_id_type=MESH,
            ),
            pltpu.make_async_remote_copy(
                s_out.at[peer_z(j), n], s_in.at[j - 1, n],
                s_send.at[j - 1, n], s_recv.at[j - 1, n],
                device_id=where, device_id_type=MESH,
            ),
        )

    beside = 1 + z // (nz - 1)
    ends = ((z == 0, (2, 1)), (z == nz - 1, (2, 3)))
    inner = jnp.logical_and(z > 0, z < nz - 1)

    def mid_copies(n):
        return tuple(
            pltpu.make_async_remote_copy(
                out.at[nz - 1 - z, n], there.at[n], m_send.at[n, a], m_recv.at[n, a],
                device_id=(beside * 2 + core, f), device_id_type=MESH,
            )
            for a, (out, there) in enumerate(((q_out, q_mid), (s_out, s_mid)))
        )

    def code(mine, v, n, i):
        top = jnp.max(jnp.max(jnp.abs(mine), axis=0), axis=0, keepdims=True)
        top = jnp.maximum(top, 1e-30)
        s_out[v, n, i:i + 1] = top * (1.0 / LEVELS)
        q_out[v, n, i] = jnp.round(mine * (LEVELS / top)).astype(jnp.int32).astype(jnp.int16)

    @pl.loop(0, chunks)
    def _(n):
        for i in range(group):
            c = n * group + i
            lhs = jnp.concatenate(
                [
                    jnp.concatenate(
                        [
                            xt[pat[c, k], :, core].reshape(nz * rows, blk),
                            xt_sib[pat[c, k]].reshape(nz * rows, blk),
                        ],
                        axis=1,
                    )
                    for k in range(slots)
                ],
                axis=0,
            )
            rhs = jnp.concatenate([g_own[:, lanes(c)], g_sib[:, lanes(c)]], axis=0)
            sums = jnp.dot(lhs, rhs, preferred_element_type=jnp.float32)
            sums = sums.reshape(slots, nz, rows, blk)
            for v in range(nz):
                mine = sums[:, v]
                terms[c, v] = mine
                code(mine, v, n, i)

        for here, js in ends:
            @pl.when(here)
            def _():
                for copy in mid_copies(n):
                    copy.start()
                for j in js:
                    for copy in z_copies(n, j):
                        copy.start()

        @pl.when(inner)
        def _():
            for j in (1, 3):
                for copy in z_copies(n, j):
                    copy.start()

    def forward(c):
        lhs = jnp.concatenate([xb[pat[c, k]] for k in range(slots)], axis=1)
        total = jnp.dot(
            lhs, w[c].reshape(slots * blk, blk), preferred_element_type=jnp.float32
        )
        out_p[:, lanes(c)] = total.astype(out_p.dtype)

    @pl.loop(0, chunks)
    def _(n):
        for i in range(group):
            forward(n * group + i)

        @pl.when(inner)
        def _():
            for copy in mid_copies(n):
                copy.wait_recv()
            to = peer_z(2)
            for i in range(group):
                came = q_mid[n, i].astype(jnp.int32).astype(jnp.float32)
                came = came * s_mid[n, i:i + 1].reshape(1, 1, blk)
                code(terms[n * group + i, to] + came, to, n, i)
            for copy in z_copies(n, 2):
                copy.start()

    for copy in scatter:
        copy.wait_recv()
    total = part[0]
    for j in range(nf - 1):
        total = total + part_in[j]
    out_t[...] = total.astype(out_t.dtype)

    def finish(n, js):
        for j in js:
            for copy in z_copies(n, j):
                copy.wait_recv()
        for i in range(group):
            c = n * group + i
            total = terms[c, z]
            for j in js:
                coded = q_in[j - 1, n, i].astype(jnp.int32).astype(jnp.float32)
                total = total + coded * s_in[j - 1, n, i:i + 1].reshape(1, 1, blk)
            out_w[c] = total * factor

    for here, js in ((z == 0, (2, 3)), (z == nz - 1, (1, 2)), (inner, (1, 2, 3))):
        @pl.when(here)
        def _():
            @pl.loop(0, chunks)
            def _(n):
                finish(n, js)

    for copy in gather + scatter + [g_swap, x_swap]:
        copy.wait_send()

    @pl.loop(0, chunks)
    def _(n):
        for here, js in ends:
            @pl.when(here)
            def _():
                for copy in mid_copies(n):
                    copy.wait_send()
                for j in js:
                    for copy in z_copies(n, j):
                        copy.wait_send()

        @pl.when(inner)
        def _():
            for j in (1, 2, 3):
                for copy in z_copies(n, j):
                    copy.wait_send()


def fused(nd, nf, tokens, weight_blocks, pattern, grad_out):
    count, width = tokens.shape
    columns, slots, blk, _ = weight_blocks.shape
    row_blocks = width * nf // blk
    entries = columns * slots
    nz = nd // 2
    rows = blk // nd
    group = 4
    chunks = columns // group
    flat = pattern.reshape(entries)
    ids = jnp.arange(entries, dtype=jnp.int32)
    keys = jnp.concatenate([flat, jnp.arange(row_blocks, dtype=jnp.int32)])
    limit = jnp.concatenate([ids, jnp.full((row_blocks,), entries, jnp.int32)])
    found = (flat[None, :] == keys[:, None]) & (ids[None, :] < limit[:, None])
    last = jnp.max(jnp.where(found, ids[None, :], -1), axis=1)
    prev = jnp.where(last < 0, entries, last)
    vmem = pl.BlockSpec(memory_space=pltpu.VMEM)
    smem = pl.BlockSpec(memory_space=pltpu.SMEM)
    hbm = pl.BlockSpec(memory_space=pl.ANY)
    dma = pltpu.SemaphoreType.DMA
    bf, f32 = jnp.bfloat16, jnp.float32
    projected, grad_tokens, grad_weight = pl.pallas_call(
        functools.partial(kernel, nf, nz, group, float((count * nd) ** -0.5)),
        out_shape=(
            jax.ShapeDtypeStruct((count, columns * blk), bf),
            jax.ShapeDtypeStruct((count, width), bf),
            jax.ShapeDtypeStruct((columns, slots, rows, blk), f32),
        ),
        in_specs=[smem, smem, hbm, hbm, hbm],
        out_specs=(vmem, vmem, vmem),
        scratch_shapes=[
            pltpu.VMEM((nf, count, width), bf),
            pltpu.VMEM((row_blocks, count, blk), bf),
            pltpu.VMEM((row_blocks, nz, 2, rows, count), bf),
            pltpu.VMEM((row_blocks, nz, rows, count), bf),
            pltpu.VMEM((count, columns * blk), bf),
            pltpu.VMEM((count, columns * blk), bf),
            pltpu.VMEM((columns, slots, blk, blk), bf),
            pltpu.VMEM((entries + 1, count, blk), f32),
            pltpu.VMEM((nf, count, width), f32),
            pltpu.VMEM((nf - 1, count, width), f32),
            pltpu.VMEM((columns, nz, slots, rows, blk), f32),
            pltpu.VMEM((nz, chunks, group, slots, rows, blk), jnp.int16),
            pltpu.VMEM((nz - 1, chunks, group, slots, rows, blk), jnp.int16),
            pltpu.VMEM((nz, chunks, 8, blk), f32),
            pltpu.VMEM((nz - 1, chunks, 8, blk), f32),
            pltpu.VMEM((chunks, group, slots, rows, blk), jnp.int16),
            pltpu.VMEM((chunks, 8, blk), f32),
            dma((3,)),
            dma((nf - 1,)), dma((nf - 1,)),
            dma((2,)), dma((2,)),
            dma((nf - 1,)), dma((nf - 1,)),
            dma((nz - 1, chunks)), dma((nz - 1, chunks)),
            dma((nz - 1, chunks)), dma((nz - 1, chunks)),
            dma((chunks, 2)), dma((chunks, 2)),
        ],
        compiler_params=pltpu.CompilerParams(
            collective_id=0, has_side_effects=True, vmem_limit_bytes=60 * 1024 * 1024
        ),
    )(pattern, prev, tokens, weight_blocks, grad_out)
    return projected, grad_tokens, grad_weight.reshape(columns, slots, rows * blk)


def solution(mesh):
    nd, nf = mesh.shape["dp"], mesh.shape["fsdp"]
    placed = (P("dp", "fsdp"), P("fsdp", None, None, None), P("fsdp", None), P("dp", "fsdp"))

    def on_device(tokens, weight_blocks, pattern, grad_out):
        columns, slots, blk, _ = weight_blocks.shape
        fits = (
            nd == 8 and blk == 128
            and tokens.shape[0] == blk and columns % 4 == 0 and nf > 1
        )
        if fits:
            return fused(nd, nf, tokens, weight_blocks, pattern, grad_out)
        return plain(tokens, weight_blocks, pattern, grad_out)

    return jax.shard_map(
        on_device,
        mesh=mesh,
        in_specs=placed,
        out_specs=(P("dp", "fsdp"), P("dp", "fsdp"), P("fsdp", None, "dp")),
        check_vma=False,
    )
```
